32 devices in a mesh: groups: 2 (over x), wide: 16 (over z, y, core).
Axes of the slice: x: 2, y: 2, z: 4, core: 2. Of those that a mesh axis runs over, the one named last changes fastest.
Arguments:
- attention_out: bfloat16 [256, 8192], P(('groups', 'wide')), parts along dimension 0, may hold values from -6 to 6
- o_weight: bfloat16 [8192, 8192], P('wide'), may hold values from -0.0625 to 0.0625
- a_down: bfloat16 [128, 64, 8192], P(('groups', 'wide')), parts along dimension 0, may hold values from -0.0625 to 0.0625
- b_up: bfloat16 [128, 64, 8192], P(('groups', 'wide')), parts along dimension 0, may hold values from -0.75 to 0.75
- adapter_home: int32 [128], P('groups'), parts along dimension 0, may hold values from 0 to 63, as said below
- req_adapter: int32 [128], P('groups'), parts along dimension 0, may hold values from 0 to 63, as said below
- req_tokens: int32 [32, 4], P('groups'), parts along dimension 0, may hold values from 1 to 4, 8 in all within a row
Outputs:
- projected: bfloat16 [256, 8192], P(('groups', 'wide')), parts along dimension 0
The draws below stay inside these ranges and needn't reach their ends.
There are 2 independent parts, one for each index of `groups`. The reference program is written for one: setup_inputs(seed, part) draws one part's arguments, and reference() takes and returns one part's arrays. A program takes and returns all parts, laid end to end along the dimension named above; an argument that names none is the same for every part. Nothing has to cross between parts.
Inputs may be any that keep to these rules, and one draw needn't show every extreme that they name: `adapter_home`: a permutation; store position p lies on the device of index p // 4 along wide. `req_adapter`: request q is held by the device of index q // 4; the adapters named by all requests include, for every keeping device, between 1 and 2 distinct adapters of its store, and exactly 2 for some device. `req_tokens`: each row sums to 8.
All inputs are finite; a program needn't handle non-finite values.
Results may differ from the reference program's by a relative error of at most 0.004.
Values may be sent and summed in bfloat16 or wider, within the bound.
No kernel may reach another device: no remote copies, remote signals or barrier semaphores. Data moves between devices by JAX's collectives and lax.ppermute only.
A program may use at most 128 MiB of HBM per device.

```python
import math
import jax
import jax.numpy as jnp
import numpy as np
from jax import lax

D = 8192
RANK = 64
TOK_DEV = 8
REQ_DEV = 4
STORE_DEV = 4
NAMED_MOST = 2
TOKENS = 128
REQUESTS = 64
ADAPTERS = 64
N_WIDE = 16


def pick_adapters(key):
    keys = jax.random.split(key, 7)
    keepers = ADAPTERS // STORE_DEV
    home = jax.random.permutation(keys[0], ADAPTERS).astype(jnp.int32)
    counts = jax.random.randint(keys[1], (keepers,), 1, NAMED_MOST + 1)
    busiest = jax.random.randint(keys[2], (), 0, keepers)
    counts = jnp.where(jnp.arange(keepers) == busiest, NAMED_MOST, counts)
    shifts = jax.random.randint(keys[3], (keepers,), 0, STORE_DEV)
    entry = jnp.arange(REQUESTS)
    leading = entry < keepers * NAMED_MOST
    keeper = jnp.where(leading, entry // NAMED_MOST, jax.random.randint(keys[4], (REQUESTS,), 0, keepers))
    keeper_count = counts[keeper]
    spare = jax.random.randint(keys[5], (REQUESTS,), 0, 1 << 20) % keeper_count
    wanted = jnp.where(leading, entry % NAMED_MOST, spare)
    local_slot = jnp.where(wanted < keeper_count, wanted, spare)
    position = keeper * STORE_DEV + (local_slot + shifts[keeper]) % STORE_DEV
    order = jax.random.permutation(keys[6], REQUESTS)
    position = position[order]
    stored = jnp.zeros((ADAPTERS,), jnp.int32).at[home].set(jnp.arange(ADAPTERS, dtype=jnp.int32))
    return (home, stored[position].astype(jnp.int32))


def draw_adapter_home(key, part):
    return pick_adapters(key)[0]


def draw_req_adapter(key, part):
    return pick_adapters(key)[1]


def block_levels(stream_key, shape, shards, least, top_value):
    loudness = 1.0
    for axis_at, blocks in shards:
        heights = jax.random.uniform(jax.random.fold_in(jax.random.fold_in(stream_key, 6), axis_at), (blocks,), jnp.float32, least / len(shards), top_value / len(shards))
        loudness = loudness * jnp.repeat(jnp.exp(heights), shape[axis_at] // blocks).reshape((-1,) + (1,) * (len(shape) - 1 - axis_at))
    return loudness


def split_up(amount, total, bound, lean):
    loads = [(1 << 20) // math.isqrt(standing ** lean) + 1 for standing in range(2, amount + 1)]
    spare, holding = total - bound - (amount - 1), [1] * (amount - 1)
    while spare > 0:
        free = [i for i in range(amount - 1) if holding[i] < bound]
        mass, left = sum([loads[i] for i in free]), spare
        for i in free:
            addition = min(bound - holding[i], max(1, left * loads[i] // mass), spare)
            holding[i] = holding[i] + addition
            spare = spare - addition
    return np.array([bound] + holding)


def ragged(stream_key, number_of, total, limit, skew):
    if number_of == 2:
        one = jax.random.randint(stream_key, (), max(1, total - limit), min(limit, total - 1) + 1)
        return jnp.stack([one, total - one])
    sizes = jnp.asarray(split_up(number_of, total, limit, skew), jnp.int32)
    couples = (number_of - 1) // 2
    giver, sink = sizes[1:1 + 2 * couples:2], sizes[2:2 + 2 * couples:2]
    slack = jnp.minimum(giver - 1, limit - sink)
    moved = jax.random.randint(jax.random.fold_in(stream_key, 1), (couples,), 0, 1 << 20) % (slack + 1)
    sizes = sizes.at[1:1 + 2 * couples:2].set(giver - moved).at[2:2 + 2 * couples:2].set(sink + moved)
    return sizes[jax.random.permutation(jax.random.fold_in(stream_key, 2), number_of)]


def gaussian(rng, extent, scale, bound, cuts=(), kind=jnp.bfloat16):
    level = block_levels(rng, extent, cuts, -0.22, 0.18) if cuts else 1.0
    result = jax.random.normal(rng, extent, jnp.float32) * scale * level
    return jnp.minimum(jnp.maximum(result, -bound), bound).astype(kind)


def setup_inputs(seed: int = 0, part: int = 0) -> dict:
    key_list = jax.random.split(jax.random.key(seed), 8)
    part_keys = jax.random.split(jax.random.fold_in(key_list[7], part), 8)
    return {
        "attention_out": gaussian(part_keys[0], (TOKENS, D), 1.0, 6.0, ((0, 16),)),
        "o_weight": gaussian(key_list[1], (D, D), D ** -0.5, 0.0625, ((0, 16),)),
        "a_down": gaussian(part_keys[2], (ADAPTERS, RANK, D), D ** -0.5, 0.0625, ((0, 16),)),
        "b_up": gaussian(part_keys[3], (ADAPTERS, RANK, D), RANK ** -0.5, 0.75, ((0, 16),)),
        "adapter_home": draw_adapter_home(jax.random.fold_in(jax.random.fold_in(key_list[7], part), 71), part),
        "req_adapter": draw_req_adapter(jax.random.fold_in(jax.random.fold_in(key_list[7], part), 71), part),
        "req_tokens": jax.vmap(lambda own: ragged(own, REQ_DEV, TOK_DEV, TOK_DEV // 2, 1))(jax.random.split(part_keys[6], N_WIDE)).reshape((N_WIDE, REQ_DEV)).astype(jnp.int32),
    }


def token_requests(req_tokens):
    request_ends = jnp.cumsum(req_tokens, axis=1)
    places = jnp.arange(TOK_DEV, dtype=jnp.int32)
    within = jnp.sum((places[None, :, None] >= request_ends[:, None, :]).astype(jnp.int32), axis=2)
    owners = jnp.arange(N_WIDE, dtype=jnp.int32)[:, None]
    return (within + owners * REQ_DEV).reshape(-1).astype(jnp.int32)


def reference(attention_out, o_weight, a_down, b_up, adapter_home, req_adapter, req_tokens):
    positions = adapter_home[req_adapter[token_requests(req_tokens)]]
    base = jnp.dot(attention_out, o_weight, preferred_element_type=jnp.float32)

    def device_rows(inputs):
        row_block, where = inputs
        a_rows = a_down[where].astype(jnp.float32)
        adapter_input = jnp.einsum("td,trd->tr", row_block.astype(jnp.float32), a_rows).astype(jnp.bfloat16)
        b_rows = b_up[where].astype(jnp.float32)
        return jnp.einsum("tr,trd->td", adapter_input.astype(jnp.float32), b_rows)

    delta = lax.map(device_rows, (attention_out.reshape(N_WIDE, TOK_DEV, D), positions.reshape(N_WIDE, TOK_DEV)))
    delta = delta.reshape(TOKENS, D)
    return (base + delta).astype(jnp.bfloat16)
```

```python
import functools

import jax
import jax.numpy as jnp
from jax import lax
from jax.experimental import pallas as pl
from jax.experimental.pallas import tpu as pltpu
from jax.sharding import Mesh, PartitionSpec as P

BF16 = jnp.bfloat16
F32 = jnp.float32
VMEM = pltpu.VMEM
SWAP = ((0, 1), (1, 0))


def other(x, axis):
    return lax.ppermute(x, axis, SWAP)


def along(x, shift):
    size = lax.axis_size("z")
    return lax.ppermute(x, "z", [(i, (i + shift) % size) for i in range(size)])


def match_table(lookup, queries):
    matches = queries[:, None] == jnp.arange(lookup.shape[0], dtype=jnp.int32)[None, :]
    return jnp.sum(jnp.where(matches, lookup[None, :], 0), axis=1)


def token_requests(req_tokens, tok_rows):
    request_ends = jnp.cumsum(req_tokens, axis=1)
    places = jnp.arange(tok_rows, dtype=jnp.int32)
    within = jnp.sum((places[None, :, None] >= request_ends[:, None, :]).astype(jnp.int32), axis=2)
    owners = jnp.arange(req_tokens.shape[0], dtype=jnp.int32)[:, None]
    return (within + owners * req_tokens.shape[1]).reshape(-1)


def partial_kernel(me_ref, slot_ref, x_ref, w_ref, a_ref, b_ref, keep_ref, send_ref, *, rank):
    rows, width = x_ref.shape
    depth = w_ref.shape[0]
    store = a_ref.shape[0]
    half = rows // 2
    inputs = lax.dot_general(x_ref[...], a_ref[...], (((1,), (1,)), ((), ())), preferred_element_type=F32)
    columns = lax.broadcasted_iota(jnp.int32, (rows, store), 1) // rank
    inputs = jnp.where(columns == slot_ref[...], inputs, 0.0).astype(BF16)
    start = pl.multiple_of(me_ref[0] * depth, depth)
    features = x_ref[:, pl.ds(start, depth)]
    step = 512

    def body(i, carry):
        at = pl.ds(pl.multiple_of(i * step, step), step)
        total = jnp.dot(features, w_ref[:, at], preferred_element_type=F32)
        total += jnp.dot(inputs, b_ref[:, at], preferred_element_type=F32)
        keep_ref[:, at] = total[:half]
        send_ref[:, at] = total[half:].astype(BF16)
        return carry

    lax.fori_loop(0, width // step, body, 0)


def partial_rows(me, slots, x, w, a, b, rank):
    rows, width = x.shape
    whole = pl.BlockSpec(memory_space=VMEM)
    held = [pltpu.with_memory_space_constraint(v, VMEM) for v in (w, a, b)]
    return pl.pallas_call(
        functools.partial(partial_kernel, rank=rank),
        out_shape=(VMEM((rows // 2, width), F32), VMEM((rows // 2, width), BF16)),
        in_specs=[pl.BlockSpec(memory_space=pltpu.SMEM)] + [whole] * 5,
        out_specs=(whole, whole),
        compiler_params=pltpu.CompilerParams(vmem_limit_bytes=8 << 20),
        name="partial_rows",
    )(me, slots, x, *held)


def shards(attention_out, o_weight, a_down, b_up, adapter_home, req_adapter, req_tokens):
    tok_rows, width = attention_out.shape
    store, rank, _ = a_down.shape
    planes = lax.axis_size("z")
    z, y, core = lax.axis_index("z"), lax.axis_index("y"), lax.axis_index("core")
    me = (z * 2 + y) * 2 + core

    zs = [attention_out] + [along(attention_out, s) for s in range(1, planes)]
    ys = [other(v, "y") for v in zs]
    mine = jnp.concatenate(zs + ys, 0)
    gathered = jnp.concatenate([mine, other(mine, "core")], 0)

    req_position = match_table(adapter_home, req_adapter)
    token_position = match_table(req_position, token_requests(req_tokens, tok_rows))
    slots = (token_position - me * store).reshape(planes, 2, 2, tok_rows)
    slots = jnp.where(core == 1, slots[:, :, ::-1], slots)
    slots = jnp.where(y == 1, slots[:, ::-1], slots)
    slots = lax.dynamic_slice_in_dim(jnp.concatenate([slots[::-1]] * 2, 0), planes - 1 - z, planes, 0)
    slots = jnp.transpose(slots, (2, 1, 0, 3)).reshape(-1, 1)

    keep, send = partial_rows(
        me.reshape(1).astype(jnp.int32), slots, gathered, o_weight,
        a_down.reshape(-1, width), b_up.reshape(-1, width), rank,
    )
    keep = keep.reshape(2, planes, tok_rows, width)
    got = other(send, "core").reshape(2, planes, tok_rows, width)
    summed = keep + got.astype(F32)
    out = summed[0, 0] + other(summed[1, 0].astype(BF16), "y").astype(F32)
    for s in range(1, planes):
        part = summed[0, s] + other(summed[1, s].astype(BF16), "y").astype(F32)
        out = out + along(part.astype(BF16), -s).astype(F32)
    return out.astype(BF16)


def solution(mesh):
    groups, wide = mesh.shape["groups"], mesh.shape["wide"]
    wide_axes = ("z", "y", "core")
    grid = Mesh(mesh.devices.reshape(groups, wide // 4, 2, 2), ("groups",) + wide_axes)
    every = ("groups",) + wide_axes
    in_specs = (
        P(every, None),
        P(wide_axes, None),
        P(every, None, None),
        P(every, None, None),
        P("groups"),
        P("groups"),
        P("groups", None),
    )
    return jax.shard_map(shards, mesh=grid, in_specs=in_specs, out_specs=P(every, None), check_vma=False)
```

```python
import functools

import jax
import jax.numpy as jnp
from jax import lax
from jax.experimental import pallas as pl
from jax.experimental.pallas import tpu as pltpu
from jax.sharding import Mesh, PartitionSpec as P

BF16 = jnp.bfloat16
F32 = jnp.float32
VMEM = pltpu.VMEM
SWAP = ((0, 1), (1, 0))
NAMED = 2
WEIGHT_COPIES = 4
WHOLE = pl.BlockSpec(memory_space=VMEM)
SCALAR = pl.BlockSpec(memory_space=pltpu.SMEM)
FAR = pl.BlockSpec(memory_space=pltpu.HBM)
PARAMS = pltpu.CompilerParams(vmem_limit_bytes=12 << 20)


def other(x, axis):
    return lax.ppermute(x, axis, SWAP)


def across(x, away):
    return lax.ppermute(x, "z", [(i, i ^ away) for i in range(lax.axis_size("z"))])


def after(x, *others):
    return lax.optimization_barrier((x, *others))[0]


def prepare_kernel(
    home_hbm, adapter_hbm, tokens_hbm, w_hbm, a_hbm, b_hbm, which_ref, w_ref, a_ref, b_ref,
    home_ref, adapter_ref, tokens_ref, table_sems, weight_sems, sems, *, tok_rows,
):
    store, rank, _ = a_hbm.shape
    requests, devices = tokens_hbm.shape
    z, y, core = lax.axis_index("z"), lax.axis_index("y"), lax.axis_index("core")
    first_position = ((z * 2 + y) * 2 + core) * store
    tables = []
    for i, (src, dst) in enumerate(((home_hbm, home_ref), (adapter_hbm, adapter_ref), (tokens_hbm, tokens_ref))):
        tables.append(pltpu.make_async_copy(src, dst, table_sems.at[i]))
    weights = []
    share = w_hbm.shape[0] // WEIGHT_COPIES
    for i in range(WEIGHT_COPIES):
        rows = pl.ds(i * share, share)
        weights.append(pltpu.make_async_copy(w_hbm.at[rows], w_ref.at[rows], weight_sems.at[i]))
    for copy in tables + weights:
        copy.start()
    for copy in tables:
        copy.wait()

    def slot_of(owner, i):
        return home_ref[adapter_ref[owner * requests + i]] - first_position

    def extremes(owner, carry):
        first, last = carry
        for i in range(requests):
            slot = slot_of(owner, i)
            here = (slot >= 0) & (slot < store)
            first = jnp.where(here, jnp.minimum(first, slot), first)
            last = jnp.where(here, jnp.maximum(last, slot), last)
        return first, last

    first, last = lax.fori_loop(0, devices, extremes, (jnp.int32(store - 1), jnp.int32(0)))
    copies = []
    for i, slot in enumerate((first, last)):
        rows = pl.ds(i * rank, rank)
        copies.append(pltpu.make_async_copy(a_hbm.at[slot], a_ref.at[rows], sems.at[2 * i]))
        copies.append(pltpu.make_async_copy(b_hbm.at[slot], b_ref.at[rows], sems.at[2 * i + 1]))
    for copy in copies:
        copy.start()

    def rows_of(owner, carry):
        block = (((owner // 4) ^ z) * 2 + ((owner % 2) ^ core)) * 2 + (((owner // 2) % 2) ^ y)
        places = lax.broadcasted_iota(jnp.int32, (tok_rows, 1), 0)
        wanted = jnp.full((tok_rows, 1), -1, jnp.int32)
        begin = jnp.int32(0)
        for i in range(requests):
            slot = slot_of(owner, i)
            one = jnp.where(slot == first, 0, jnp.where(slot == last, 1, -1))
            wanted = jnp.where(places >= begin, one, wanted)
            begin = begin + tokens_ref[i, owner]
        which_ref[pl.ds(pl.multiple_of(block * tok_rows, tok_rows), tok_rows), :] = wanted
        return carry

    lax.fori_loop(0, devices, rows_of, 0)
    for copy in copies + weights:
        copy.wait()


def prepare(home, adapter, tokens, w, a, b, tok_rows):
    _, rank, width = a.shape
    rows = tokens.shape[0] * tok_rows
    sources = (home, adapter, tokens.T, w, a, b)
    return pl.pallas_call(
        functools.partial(prepare_kernel, tok_rows=tok_rows),
        out_shape=(
            VMEM((rows, 1), jnp.int32),
            VMEM(w.shape, BF16),
            VMEM((NAMED * rank, width), BF16),
            VMEM((NAMED * rank, width), BF16),
        ),
        in_specs=[FAR] * len(sources),
        out_specs=(WHOLE,) * 4,
        scratch_shapes=[pltpu.SMEM(v.shape, jnp.int32) for v in sources[:3]]
        + [pltpu.SemaphoreType.DMA((n,)) for n in (3, WEIGHT_COPIES, 2 * NAMED)],
        compiler_params=PARAMS,
        cost_estimate=pl.CostEstimate(flops=0, bytes_accessed=12 << 20, transcendentals=0),
        name="prepare",
    )(*[pltpu.with_memory_space_constraint(v, pltpu.HBM) for v in sources])


def partial_kernel(which_ref, w_ref, a_ref, b_ref, *refs, parts, rank):
    xs, outs, x_ref = refs[: 4 * len(parts)], refs[4 * len(parts) : -1], refs[-1]
    tok_rows, width = xs[0].shape
    depth = w_ref.shape[0]
    step = 2048
    me = (lax.axis_index("z") * 2 + lax.axis_index("y")) * 2 + lax.axis_index("core")

    inputs = None
    for k in range(0, width, step):
        at = pl.ds(k, step)
        rows = jnp.concatenate([x[:, at].astype(F32) for x in xs], 0).astype(BF16)
        x_ref[:, at] = rows
        part = lax.dot_general(rows, a_ref[:, at], (((1,), (1,)), ((), ())), preferred_element_type=F32)
        inputs = part if inputs is None else inputs + part
    block = 4 * tok_rows
    which = jnp.concatenate([which_ref[pl.ds(s * block, block), :] for s in parts], 0)
    columns = lax.broadcasted_iota(jnp.int32, inputs.shape, 1) // rank
    inputs = jnp.where(columns == which, inputs, 0.0).astype(BF16)
    features = x_ref[:, pl.ds(pl.multiple_of(me * depth, depth), depth)]

    def body(i, carry):
        at = pl.ds(pl.multiple_of(i * step, step), step)
        total = jnp.dot(features, w_ref[:, at], preferred_element_type=F32)
        total += jnp.dot(inputs, b_ref[:, at], preferred_element_type=F32)
        half = block // 2
        for j in range(len(parts)):
            outs[2 * j][:, at] = total[j * block : j * block + half]
            outs[2 * j + 1][:, at] = total[j * block + half : (j + 1) * block].astype(BF16)
        return carry

    lax.fori_loop(0, width // step, body, 0)


def partial_rows(which, w, a, b, xs, parts, rank):
    rows, width = xs[0].shape
    held = [pltpu.with_memory_space_constraint(v, VMEM) for v in (which, w, a, b, *xs)]
    total = 4 * rows * len(parts)
    return pl.pallas_call(
        functools.partial(partial_kernel, parts=parts, rank=rank),
        out_shape=(VMEM((2 * rows, width), F32), VMEM((2 * rows, width), BF16)) * len(parts),
        in_specs=[WHOLE] * len(held),
        out_specs=(WHOLE,) * (2 * len(parts)),
        scratch_shapes=[VMEM((total, width), BF16)],
        compiler_params=PARAMS,
        cost_estimate=pl.CostEstimate(
            flops=2 * total * width * (w.shape[0] + 2 * a.shape[0]), bytes_accessed=16 << 20, transcendentals=0
        ),
        name="partial_rows",
    )(*held)


def shards(attention_out, o_weight, a_down, b_up, adapter_home, req_adapter, req_tokens):
    tok_rows, width = attention_out.shape
    rank = a_down.shape[1]
    planes = lax.axis_size("z")
    which, w, a, b = prepare(adapter_home, req_adapter, req_tokens, o_weight, a_down, b_up, tok_rows)

    far = {0: attention_out, 1: across(attention_out, 1)}
    for e in range(2, planes, 2):
        far[e] = after(across(attention_out, e), which)
        far[e + 1] = across(far[e], 1)
    near = {e: other(far[e], "y") for e in range(planes)}

    parts = tuple(range(planes))[::-1]
    xs = []
    for e in parts:
        xs += [far[e], near[e], other(far[e], "core"), other(near[e], "core")]
    sums = partial_rows(which, w, a, b, xs, parts, rank)
    out = None
    arriving = []
    before = ()
    for j, e in enumerate(parts):
        keep, got = sums[2 * j], other(sums[2 * j + 1], "core")
        here = keep[:tok_rows] + got[:tok_rows].astype(F32)
        there = (keep[tok_rows:] + got[tok_rows:].astype(F32)).astype(BF16)
        if e == 0:
            there = after(there, *before)
        received = other(there, "y")
        if e > 1:
            before = (received,)
        part = here + received.astype(F32)
        if e == 0:
            out = part
        else:
            arriving.append(across(part.astype(BF16), e))
    for part in arriving:
        out = out + part.astype(F32)
    return out.astype(BF16)


def solution(mesh):
    groups, wide = mesh.shape["groups"], mesh.shape["wide"]
    wide_axes = ("z", "y", "core")
    grid = Mesh(mesh.devices.reshape(groups, wide // 4, 2, 2), ("groups",) + wide_axes)
    every = ("groups",) + wide_axes
    in_specs = (
        P(every, None),
        P(wide_axes, None),
        P(every, None, None),
        P(every, None, None),
        P("groups"),
        P("groups"),
        P("groups", None),
    )
    return jax.shard_map(shards, mesh=grid, in_specs=in_specs, out_specs=P(every, None), check_vma=False)
```

```python
import functools

import jax
import jax.numpy as jnp
from jax import lax
from jax.experimental import pallas as pl
from jax.experimental.pallas import tpu as pltpu
from jax.sharding import Mesh, PartitionSpec as P

BF16 = jnp.bfloat16
F32 = jnp.float32
VMEM = pltpu.VMEM
SWAP = ((0, 1), (1, 0))
NAMED = 2
WHOLE = pl.BlockSpec(memory_space=VMEM)
SCALAR = pl.BlockSpec(memory_space=pltpu.SMEM)
FAR = pl.BlockSpec(memory_space=pltpu.HBM)
PARAMS = pltpu.CompilerParams(vmem_limit_bytes=24 << 20)


def other(x, axis):
    return lax.ppermute(x, axis, SWAP)


def across(x, away):
    return lax.ppermute(x, "z", [(i, i ^ away) for i in range(lax.axis_size("z"))])


def after(x, *others):
    return lax.optimization_barrier((x, *others))[0]


def prepare_kernel(
    home_hbm, adapter_hbm, tokens_hbm, a_hbm, b_hbm, x_hbm, which_ref, a_ref, b_ref, x_ref,
    home_ref, adapter_ref, tokens_ref, table_sems, sems, *, tok_rows,
):
    store, rank, _ = a_hbm.shape
    requests, devices = tokens_hbm.shape
    z, y, core = lax.axis_index("z"), lax.axis_index("y"), lax.axis_index("core")
    first_position = ((z * 2 + y) * 2 + core) * store
    tables = []
    for i, (src, dst) in enumerate(((home_hbm, home_ref), (adapter_hbm, adapter_ref), (tokens_hbm, tokens_ref))):
        tables.append(pltpu.make_async_copy(src, dst, table_sems.at[i]))
    own = pltpu.make_async_copy(x_hbm, x_ref, sems.at[2 * NAMED])
    for copy in (*tables, own):
        copy.start()
    for copy in tables:
        copy.wait()

    def slot_of(owner, i):
        return home_ref[adapter_ref[owner * requests + i]] - first_position

    def extremes(owner, carry):
        first, last = carry
        for i in range(requests):
            slot = slot_of(owner, i)
            here = (slot >= 0) & (slot < store)
            first = jnp.where(here, jnp.minimum(first, slot), first)
            last = jnp.where(here, jnp.maximum(last, slot), last)
        return first, last

    first, last = lax.fori_loop(0, devices, extremes, (jnp.int32(store - 1), jnp.int32(0)))
    copies = []
    for i, slot in enumerate((first, last)):
        rows = pl.ds(i * rank, rank)
        copies.append(pltpu.make_async_copy(a_hbm.at[slot], a_ref.at[rows], sems.at[2 * i]))
        copies.append(pltpu.make_async_copy(b_hbm.at[slot], b_ref.at[rows], sems.at[2 * i + 1]))
    for copy in copies:
        copy.start()

    def rows_of(owner, carry):
        block = (((owner // 4) ^ z) * 2 + ((owner % 2) ^ core)) * 2 + (((owner // 2) % 2) ^ y)
        places = lax.broadcasted_iota(jnp.int32, (tok_rows, 1), 0)
        wanted = jnp.full((tok_rows, 1), -1, jnp.int32)
        begin = jnp.int32(0)
        for i in range(requests):
            slot = slot_of(owner, i)
            one = jnp.where(slot == first, 0, jnp.where(slot == last, 1, -1))
            wanted = jnp.where(places >= begin, one, wanted)
            begin = begin + tokens_ref[i, owner]
        which_ref[pl.ds(pl.multiple_of(block * tok_rows, tok_rows), tok_rows), :] = wanted
        return carry

    lax.fori_loop(0, devices, rows_of, 0)
    for copy in (*copies, own):
        copy.wait()


def prepare(home, adapter, tokens, a, b, x, tok_rows):
    _, rank, width = a.shape
    rows = tokens.shape[0] * tok_rows
    sources = (home, adapter, tokens.T, a, b, x)
    return pl.pallas_call(
        functools.partial(prepare_kernel, tok_rows=tok_rows),
        out_shape=(
            VMEM((rows, 1), jnp.int32),
            VMEM((NAMED * rank, width), BF16),
            VMEM((NAMED * rank, width), BF16),
            VMEM(x.shape, BF16),
        ),
        in_specs=[FAR] * len(sources),
        out_specs=(WHOLE,) * 4,
        scratch_shapes=[pltpu.SMEM(v.shape, jnp.int32) for v in sources[:3]]
        + [pltpu.SemaphoreType.DMA((n,)) for n in (3, 2 * NAMED + 1)],
        compiler_params=PARAMS,
        cost_estimate=pl.CostEstimate(flops=0, bytes_accessed=4 << 20, transcendentals=0),
        name="prepare",
    )(*[pltpu.with_memory_space_constraint(v, pltpu.HBM) for v in sources])


def partial_kernel(which_ref, w_ref, a_ref, b_ref, *refs, parts, rank):
    xs, outs, x_ref = refs[: 4 * len(parts)], refs[4 * len(parts) : -1], refs[-1]
    tok_rows, width = xs[0].shape
    depth = w_ref.shape[0]
    step = 2048
    me = (lax.axis_index("z") * 2 + lax.axis_index("y")) * 2 + lax.axis_index("core")

    inputs = None
    for k in range(0, width, step):
        at = pl.ds(k, step)
        rows = jnp.concatenate([x[:, at].astype(F32) for x in xs], 0).astype(BF16)
        x_ref[:, at] = rows
        part = lax.dot_general(rows, a_ref[:, at], (((1,), (1,)), ((), ())), preferred_element_type=F32)
        inputs = part if inputs is None else inputs + part
    block = 4 * tok_rows
    which = jnp.concatenate([which_ref[pl.ds(s * block, block), :] for s in parts], 0)
    columns = lax.broadcasted_iota(jnp.int32, inputs.shape, 1) // rank
    inputs = jnp.where(columns == which, inputs, 0.0).astype(BF16)
    features = x_ref[:, pl.ds(pl.multiple_of(me * depth, depth), depth)]

    def body(i, carry):
        at = pl.ds(pl.multiple_of(i * step, step), step)
        total = jnp.dot(features, w_ref[:, at], preferred_element_type=F32)
        total += jnp.dot(inputs, b_ref[:, at], preferred_element_type=F32)
        half = block // 2
        for j in range(len(parts)):
            outs[2 * j][:, at] = total[j * block : j * block + half]
            outs[2 * j + 1][:, at] = total[j * block + half : (j + 1) * block].astype(BF16)
        return carry

    lax.fori_loop(0, width // step, body, 0)


def partial_rows(which, w, a, b, xs, parts, rank):
    rows, width = xs[0].shape
    which, a, b, *xs = [pltpu.with_memory_space_constraint(v, VMEM) for v in (which, a, b, *xs)]
    total = 4 * rows * len(parts)
    return pl.pallas_call(
        functools.partial(partial_kernel, parts=parts, rank=rank),
        out_shape=(VMEM((2 * rows, width), F32), VMEM((2 * rows, width), BF16)) * len(parts),
        in_specs=[WHOLE] * (4 + len(xs)),
        out_specs=(WHOLE,) * (2 * len(parts)),
        scratch_shapes=[VMEM((total, width), BF16)],
        compiler_params=PARAMS,
        cost_estimate=pl.CostEstimate(
            flops=2 * total * width * (w.shape[0] + 2 * a.shape[0]), bytes_accessed=16 << 20, transcendentals=0
        ),
        name="partial_rows",
    )(which, w, a, b, *xs)


def shards(attention_out, o_weight, a_down, b_up, adapter_home, req_adapter, req_tokens):
    tok_rows, width = attention_out.shape
    rank = a_down.shape[1]
    planes = lax.axis_size("z")
    which, a, b, own = prepare(adapter_home, req_adapter, req_tokens, a_down, b_up, attention_out, tok_rows)

    far = {0: attention_out, 1: across(attention_out, 1)}
    for e in range(2, planes, 2):
        far[e] = after(across(attention_out, e), which)
        far[e + 1] = across(far[e], 1)
    near = {e: other(far[e], "y") for e in range(planes)}

    parts = tuple(range(planes))[::-1]
    xs = []
    for e in parts:
        xs += [far[e] if e else own, near[e], other(far[e], "core"), other(near[e], "core")]
    sums = partial_rows(which, o_weight, a, b, xs, parts, rank)
    out = None
    arriving = []
    before = ()
    for j, e in enumerate(parts):
        keep, got = sums[2 * j], other(sums[2 * j + 1], "core")
        here = keep[:tok_rows] + got[:tok_rows].astype(F32)
        there = (keep[tok_rows:] + got[tok_rows:].astype(F32)).astype(BF16)
        if e == 0:
            there = after(there, *before)
        received = other(there, "y")
        if e > 1:
            before = (received,)
        part = here + received.astype(F32)
        if e == 0:
            out = part
        else:
            arriving.append(across(part.astype(BF16), e))
    for part in arriving:
        out = out + part.astype(F32)
    return out.astype(BF16)


def solution(mesh):
    groups, wide = mesh.shape["groups"], mesh.shape["wide"]
    wide_axes = ("z", "y", "core")
    grid = Mesh(mesh.devices.reshape(groups, wide // 4, 2, 2), ("groups",) + wide_axes)
    every = ("groups",) + wide_axes
    in_specs = (
        P(every, None),
        P(wide_axes, None),
        P(every, None, None),
        P(every, None, None),
        P("groups"),
        P("groups"),
        P("groups", None),
    )
    return jax.shard_map(shards, mesh=grid, in_specs=in_specs, out_specs=P(every, None), check_vma=False)
```

```python
import functools

import jax
import jax.numpy as jnp
from jax import lax
from jax.experimental import pallas as pl
from jax.experimental.pallas import tpu as pltpu
from jax.sharding import Mesh, PartitionSpec as P

BF16 = jnp.bfloat16
F32 = jnp.float32
VMEM = pltpu.VMEM
SWAP = ((0, 1), (1, 0))
NAMED = 2
WHOLE = pl.BlockSpec(memory_space=VMEM)
SCALAR = pl.BlockSpec(memory_space=pltpu.SMEM)
FAR = pl.BlockSpec(memory_space=pltpu.HBM)
PARAMS = pltpu.CompilerParams(vmem_limit_bytes=24 << 20)


def other(x, axis):
    return lax.ppermute(x, axis, SWAP)


def across(x, away):
    return lax.ppermute(x, "z", [(i, i ^ away) for i in range(lax.axis_size("z"))])


def after(x, *others):
    return lax.optimization_barrier((x, *others))[0]


def prepare_kernel(
    home_hbm, adapter_hbm, tokens_hbm, a_hbm, b_hbm, x_hbm, which_ref, a_ref, b_ref, x_ref,
    home_ref, adapter_ref, tokens_ref, table_sems, sems, *, tok_rows,
):
    store, rank, _ = a_hbm.shape
    requests, devices = tokens_hbm.shape
    z, y, core = lax.axis_index("z"), lax.axis_index("y"), lax.axis_index("core")
    first_position = ((z * 2 + y) * 2 + core) * store
    tables = []
    for i, (src, dst) in enumerate(((home_hbm, home_ref), (adapter_hbm, adapter_ref), (tokens_hbm, tokens_ref))):
        tables.append(pltpu.make_async_copy(src, dst, table_sems.at[i]))
    own = pltpu.make_async_copy(x_hbm, x_ref, sems.at[2 * NAMED])
    for copy in (*tables, own):
        copy.start()
    for copy in tables:
        copy.wait()

    def slot_of(owner, i):
        return home_ref[adapter_ref[owner * requests + i]] - first_position

    def extremes(owner, carry):
        first, last = carry
        for i in range(requests):
            slot = slot_of(owner, i)
            here = (slot >= 0) & (slot < store)
            first = jnp.where(here, jnp.minimum(first, slot), first)
            last = jnp.where(here, jnp.maximum(last, slot), last)
        return first, last

    first, last = lax.fori_loop(0, devices, extremes, (jnp.int32(store - 1), jnp.int32(0)))
    copies = []
    for i, slot in enumerate((first, last)):
        rows = pl.ds(i * rank, rank)
        copies.append(pltpu.make_async_copy(a_hbm.at[slot], a_ref.at[rows], sems.at[2 * i]))
        copies.append(pltpu.make_async_copy(b_hbm.at[slot], b_ref.at[rows], sems.at[2 * i + 1]))
    for copy in copies:
        copy.start()

    def rows_of(owner, carry):
        block = (((owner // 4) ^ z) * 2 + ((owner % 2) ^ core)) * 2 + (((owner // 2) % 2) ^ y)
        places = lax.broadcasted_iota(jnp.int32, (tok_rows, 1), 0)
        wanted = jnp.full((tok_rows, 1), -1, jnp.int32)
        begin = jnp.int32(0)
        for i in range(requests):
            slot = slot_of(owner, i)
            one = jnp.where(slot == first, 0, jnp.where(slot == last, 1, -1))
            wanted = jnp.where(places >= begin, one, wanted)
            begin = begin + tokens_ref[i, owner]
        which_ref[pl.ds(pl.multiple_of(block * tok_rows, tok_rows), tok_rows), :] = wanted
        return carry

    lax.fori_loop(0, devices, rows_of, 0)
    for copy in (*copies, own):
        copy.wait()


def prepare(home, adapter, tokens, a, b, x, tok_rows):
    _, rank, width = a.shape
    rows = tokens.shape[0] * tok_rows
    sources = (home, adapter, tokens.T, a, b, x)
    return pl.pallas_call(
        functools.partial(prepare_kernel, tok_rows=tok_rows),
        out_shape=(
            VMEM((rows, 1), jnp.int32),
            VMEM((NAMED * rank, width), BF16),
            VMEM((NAMED * rank, width), BF16),
            VMEM(x.shape, BF16),
        ),
        in_specs=[FAR] * len(sources),
        out_specs=(WHOLE,) * 4,
        scratch_shapes=[pltpu.SMEM(v.shape, jnp.int32) for v in sources[:3]]
        + [pltpu.SemaphoreType.DMA((n,)) for n in (3, 2 * NAMED + 1)],
        compiler_params=PARAMS,
        cost_estimate=pl.CostEstimate(flops=0, bytes_accessed=4 << 20, transcendentals=0),
        name="prepare",
    )(*[pltpu.with_memory_space_constraint(v, pltpu.HBM) for v in sources])


def partial_kernel(which_ref, w_ref, a_ref, b_ref, *refs, parts, rank):
    xs, outs, x_ref = refs[: 4 * len(parts)], refs[4 * len(parts) : -1], refs[-1]
    tok_rows, width = xs[0].shape
    depth = w_ref.shape[0]
    step = 2048
    me = (lax.axis_index("z") * 2 + lax.axis_index("y")) * 2 + lax.axis_index("core")

    inputs = None
    for k in range(0, width, step):
        at = pl.ds(k, step)
        rows = jnp.concatenate([x[:, at].astype(F32) for x in xs], 0).astype(BF16)
        x_ref[:, at] = rows
        part = lax.dot_general(rows, a_ref[:, at], (((1,), (1,)), ((), ())), preferred_element_type=F32)
        inputs = part if inputs is None else inputs + part
    block = 4 * tok_rows
    which = jnp.concatenate([which_ref[pl.ds(s * block, block), :] for s in parts], 0)
    columns = lax.broadcasted_iota(jnp.int32, inputs.shape, 1) // rank
    inputs = jnp.where(columns == which, inputs, 0.0).astype(BF16)
    features = x_ref[:, pl.ds(pl.multiple_of(me * depth, depth), depth)]

    def body(i, carry):
        at = pl.ds(pl.multiple_of(i * step, step), step)
        total = jnp.dot(features, w_ref[:, at], preferred_element_type=F32)
        total += jnp.dot(inputs, b_ref[:, at], preferred_element_type=F32)
        half = block // 2
        for j in range(len(parts)):
            outs[2 * j][:, at] = total[j * block : j * block + half]
            outs[2 * j + 1][:, at] = total[j * block + half : (j + 1) * block].astype(BF16)
        return carry

    lax.fori_loop(0, width // step, body, 0)


def partial_rows(which, w, a, b, xs, parts, rank):
    rows, width = xs[0].shape
    which, a, b, *xs = [pltpu.with_memory_space_constraint(v, VMEM) for v in (which, a, b, *xs)]
    total = 4 * rows * len(parts)
    return pl.pallas_call(
        functools.partial(partial_kernel, parts=parts, rank=rank),
        out_shape=(VMEM((2 * rows, width), F32), VMEM((2 * rows, width), BF16)) * len(parts),
        in_specs=[WHOLE] * (4 + len(xs)),
        out_specs=(WHOLE,) * (2 * len(parts)),
        scratch_shapes=[VMEM((total, width), BF16)],
        compiler_params=PARAMS,
        cost_estimate=pl.CostEstimate(
            flops=2 * total * width * (w.shape[0] + 2 * a.shape[0]), bytes_accessed=16 << 20, transcendentals=0
        ),
        name="partial_rows",
    )(which, w, a, b, *xs)


def shards(attention_out, o_weight, a_down, b_up, adapter_home, req_adapter, req_tokens):
    tok_rows, width = attention_out.shape
    rank = a_down.shape[1]
    planes = lax.axis_size("z")
    which, a, b, own = prepare(adapter_home, req_adapter, req_tokens, a_down, b_up, attention_out, tok_rows)

    far = {0: attention_out, 1: across(attention_out, 1)}
    near = {e: other(far[e], "y") for e in range(2)}
    for e in range(2, planes, 2):
        far[e] = after(across(attention_out, e), which)
        near[e] = other(far[e], "y")
        far[e + 1], near[e + 1] = across(far[e], 1), across(near[e], 1)

    parts = tuple(range(planes))[::-1]
    xs = []
    for e in parts:
        xs += [far[e] if e else own, near[e], other(far[e], "core"), other(near[e], "core")]
    sums = partial_rows(which, o_weight, a, b, xs, parts, rank)
    out = None
    arriving = []
    before = ()
    for j, e in enumerate(parts):
        keep, got = sums[2 * j], other(sums[2 * j + 1], "core")
        here = keep[:tok_rows] + got[:tok_rows].astype(F32)
        there = (keep[tok_rows:] + got[tok_rows:].astype(F32)).astype(BF16)
        if e == 0:
            there = after(there, *before)
        received = other(there, "y")
        if e > 1:
            before = (received,)
        part = here + received.astype(F32)
        if e == 0:
            out = part
        else:
            arriving.append(across(part.astype(BF16), e))
    for part in arriving:
        out = out + part.astype(F32)
    return out.astype(BF16)


def solution(mesh):
    groups, wide = mesh.shape["groups"], mesh.shape["wide"]
    wide_axes = ("z", "y", "core")
    grid = Mesh(mesh.devices.reshape(groups, wide // 4, 2, 2), ("groups",) + wide_axes)
    every = ("groups",) + wide_axes
    in_specs = (
        P(every, None),
        P(wide_axes, None),
        P(every, None, None),
        P(every, None, None),
        P("groups"),
        P("groups"),
        P("groups", None),
    )
    return jax.shard_map(shards, mesh=grid, in_specs=in_specs, out_specs=P(every, None), check_vma=False)
```

```python
import functools

import jax
import jax.numpy as jnp
from jax import lax
from jax.experimental import pallas as pl
from jax.experimental.pallas import tpu as pltpu
from jax.sharding import Mesh, PartitionSpec as P

BF16 = jnp.bfloat16
F32 = jnp.float32
VMEM = pltpu.VMEM
SWAP = ((0, 1), (1, 0))
NAMED = 2
WHOLE = pl.BlockSpec(memory_space=VMEM)
SCALAR = pl.BlockSpec(memory_space=pltpu.SMEM)
FAR = pl.BlockSpec(memory_space=pltpu.HBM)
PARAMS = pltpu.CompilerParams(vmem_limit_bytes=24 << 20)


def other(x, axis):
    return lax.ppermute(x, axis, SWAP)


def across(x, away):
    return lax.ppermute(x, "z", [(i, i ^ away) for i in range(lax.axis_size("z"))])


def after(x, *others):
    return lax.optimization_barrier((x, *others))[0]


def prepare_kernel(
    home_hbm, adapter_hbm, tokens_hbm, a_hbm, b_hbm, x_hbm, which_ref, a_ref, b_ref, x_ref,
    home_ref, adapter_ref, tokens_ref, table_sems, sems, *, tok_rows,
):
    store, rank, _ = a_hbm.shape
    requests, devices = tokens_hbm.shape
    z, y, core = lax.axis_index("z"), lax.axis_index("y"), lax.axis_index("core")
    first_position = ((z * 2 + y) * 2 + core) * store
    tables = []
    for i, (src, dst) in enumerate(((home_hbm, home_ref), (adapter_hbm, adapter_ref), (tokens_hbm, tokens_ref))):
        tables.append(pltpu.make_async_copy(src, dst, table_sems.at[i]))
    own = pltpu.make_async_copy(x_hbm, x_ref, sems.at[2 * NAMED])
    for copy in (*tables, own):
        copy.start()
    for copy in tables:
        copy.wait()

    def slot_of(owner, i):
        return home_ref[adapter_ref[owner * requests + i]] - first_position

    def extremes(owner, carry):
        first, last = carry
        for i in range(requests):
            slot = slot_of(owner, i)
            here = (slot >= 0) & (slot < store)
            first = jnp.where(here, jnp.minimum(first, slot), first)
            last = jnp.where(here, jnp.maximum(last, slot), last)
        return first, last

    first, last = lax.fori_loop(0, devices, extremes, (jnp.int32(store - 1), jnp.int32(0)))
    copies = []
    for i, slot in enumerate((first, last)):
        rows = pl.ds(i * rank, rank)
        copies.append(pltpu.make_async_copy(a_hbm.at[slot], a_ref.at[rows], sems.at[2 * i]))
        copies.append(pltpu.make_async_copy(b_hbm.at[slot], b_ref.at[rows], sems.at[2 * i + 1]))
    for copy in copies:
        copy.start()

    def rows_of(owner, carry):
        block = (((owner // 4) ^ z) * 2 + ((owner % 2) ^ core)) * 2 + (((owner // 2) % 2) ^ y)
        places = lax.broadcasted_iota(jnp.int32, (tok_rows, 1), 0)
        wanted = jnp.full((tok_rows, 1), -1, jnp.int32)
        begin = jnp.int32(0)
        for i in range(requests):
            slot = slot_of(owner, i)
            one = jnp.where(slot == first, 0, jnp.where(slot == last, 1, -1))
            wanted = jnp.where(places >= begin, one, wanted)
            begin = begin + tokens_ref[i, owner]
        which_ref[pl.ds(pl.multiple_of(block * tok_rows, tok_rows), tok_rows), :] = wanted
        return carry

    lax.fori_loop(0, devices, rows_of, 0)
    for copy in (*copies, own):
        copy.wait()


def prepare(home, adapter, tokens, a, b, x, tok_rows):
    _, rank, width = a.shape
    rows = tokens.shape[0] * tok_rows
    sources = (home, adapter, tokens.T, a, b, x)
    return pl.pallas_call(
        functools.partial(prepare_kernel, tok_rows=tok_rows),
        out_shape=(
            VMEM((rows, 1), jnp.int32),
            VMEM((NAMED * rank, width), BF16),
            VMEM((NAMED * rank, width), BF16),
            VMEM(x.shape, BF16),
        ),
        in_specs=[FAR] * len(sources),
        out_specs=(WHOLE,) * 4,
        scratch_shapes=[pltpu.SMEM(v.shape, jnp.int32) for v in sources[:3]]
        + [pltpu.SemaphoreType.DMA((n,)) for n in (3, 2 * NAMED + 1)],
        compiler_params=PARAMS,
        cost_estimate=pl.CostEstimate(flops=0, bytes_accessed=4 << 20, transcendentals=0),
        name="prepare",
    )(*[pltpu.with_memory_space_constraint(v, pltpu.HBM) for v in sources])


def partial_kernel(which_ref, w_ref, a_ref, b_ref, *refs, parts, rank):
    xs, outs, x_ref = refs[: 4 * len(parts)], refs[4 * len(parts) : -1], refs[-1]
    tok_rows, width = xs[0].shape
    depth = w_ref.shape[0]
    step = 4096
    me = (lax.axis_index("z") * 2 + lax.axis_index("y")) * 2 + lax.axis_index("core")

    inputs = None
    for k in range(0, width, step):
        at = pl.ds(k, step)
        rows = jnp.concatenate([x[:, at].astype(F32) for x in xs], 0).astype(BF16)
        x_ref[:, at] = rows
        part = lax.dot_general(rows, a_ref[:, at], (((1,), (1,)), ((), ())), preferred_element_type=F32)
        inputs = part if inputs is None else inputs + part
    block = 4 * tok_rows
    which = jnp.concatenate([which_ref[pl.ds(s * block, block), :] for s in parts], 0)
    columns = lax.broadcasted_iota(jnp.int32, inputs.shape, 1) // rank
    inputs = jnp.where(columns == which, inputs, 0.0).astype(BF16)
    features = x_ref[:, pl.ds(pl.multiple_of(me * depth, depth), depth)]

    def body(i, carry):
        at = pl.ds(pl.multiple_of(i * step, step), step)
        total = jnp.dot(features, w_ref[:, at], preferred_element_type=F32)
        total += jnp.dot(inputs, b_ref[:, at], preferred_element_type=F32)
        half = block // 2
        for j in range(len(parts)):
            outs[2 * j][:, at] = total[j * block : j * block + half]
            outs[2 * j + 1][:, at] = total[j * block + half : (j + 1) * block].astype(BF16)
        return carry

    lax.fori_loop(0, width // step, body, 0)


def partial_rows(which, w, a, b, xs, parts, rank):
    rows, width = xs[0].shape
    which, a, b, *xs = [pltpu.with_memory_space_constraint(v, VMEM) for v in (which, a, b, *xs)]
    total = 4 * rows * len(parts)
    return pl.pallas_call(
        functools.partial(partial_kernel, parts=parts, rank=rank),
        out_shape=(VMEM((2 * rows, width), F32), VMEM((2 * rows, width), BF16)) * len(parts),
        in_specs=[WHOLE] * (4 + len(xs)),
        out_specs=(WHOLE,) * (2 * len(parts)),
        scratch_shapes=[VMEM((total, width), BF16)],
        compiler_params=PARAMS,
        cost_estimate=pl.CostEstimate(
            flops=2 * total * width * (w.shape[0] + 2 * a.shape[0]), bytes_accessed=16 << 20, transcendentals=0
        ),
        name="partial_rows",
    )(which, w, a, b, *xs)


def shards(attention_out, o_weight, a_down, b_up, adapter_home, req_adapter, req_tokens):
    tok_rows, width = attention_out.shape
    rank = a_down.shape[1]
    planes = lax.axis_size("z")
    which, a, b, own = prepare(adapter_home, req_adapter, req_tokens, a_down, b_up, attention_out, tok_rows)

    far = {0: attention_out, 1: across(attention_out, 1)}
    near = {e: other(far[e], "y") for e in range(2)}
    for e in range(2, planes, 2):
        far[e] = after(across(attention_out, e), which)
        near[e] = other(far[e], "y")
        far[e + 1], near[e + 1] = across(far[e], 1), across(near[e], 1)

    parts = tuple(range(planes))[::-1]
    xs = []
    for e in parts:
        xs += [far[e] if e else own, near[e], other(far[e], "core"), other(near[e], "core")]
    sums = partial_rows(which, o_weight, a, b, xs, parts, rank)
    out = None
    arriving = []
    before = ()
    for j, e in enumerate(parts):
        keep, got = sums[2 * j], other(sums[2 * j + 1], "core")
        here = keep[:tok_rows] + got[:tok_rows].astype(F32)
        there = (keep[tok_rows:] + got[tok_rows:].astype(F32)).astype(BF16)
        if e == 0:
            there = after(there, *before)
        received = other(there, "y")
        if e > 1:
            before = (received,)
        part = here + received.astype(F32)
        if e == 0:
            out = part
        else:
            arriving.append(across(part.astype(BF16), e))
    for part in arriving:
        out = out + part.astype(F32)
    return out.astype(BF16)


def solution(mesh):
    groups, wide = mesh.shape["groups"], mesh.shape["wide"]
    wide_axes = ("z", "y", "core")
    grid = Mesh(mesh.devices.reshape(groups, wide // 4, 2, 2), ("groups",) + wide_axes)
    every = ("groups",) + wide_axes
    in_specs = (
        P(every, None),
        P(wide_axes, None),
        P(every, None, None),
        P(every, None, None),
        P("groups"),
        P("groups"),
        P("groups", None),
    )
    return jax.shard_map(shards, mesh=grid, in_specs=in_specs, out_specs=P(every, None), check_vma=False)
```

```python
import functools

import jax
import jax.numpy as jnp
from jax import lax
from jax.experimental import pallas as pl
from jax.experimental.pallas import tpu as pltpu
from jax.sharding import Mesh, PartitionSpec as P

BF16 = jnp.bfloat16
F32 = jnp.float32
VMEM = pltpu.VMEM
SWAP = ((0, 1), (1, 0))
NAMED = 2
WHOLE = pl.BlockSpec(memory_space=VMEM)
SCALAR = pl.BlockSpec(memory_space=pltpu.SMEM)
FAR = pl.BlockSpec(memory_space=pltpu.HBM)
PARAMS = pltpu.CompilerParams(vmem_limit_bytes=24 << 20)


def other(x, axis):
    return lax.ppermute(x, axis, SWAP)


def across(x, away):
    return lax.ppermute(x, "z", [(i, i ^ away) for i in range(lax.axis_size("z"))])


def diagonal(x, away):
    places = [(i, j) for i in range(lax.axis_size("z")) for j in range(2)]
    return lax.ppermute(x, ("z", "y"), [(2 * i + j, 2 * (i ^ away) + 1 - j) for i, j in places])


def after(x, *others):
    return lax.optimization_barrier((x, *others))[0]


def prepare_kernel(
    home_hbm, adapter_hbm, tokens_hbm, a_hbm, b_hbm, x_hbm, which_ref, a_ref, b_ref, x_ref,
    home_ref, adapter_ref, tokens_ref, table_sems, sems, *, tok_rows,
):
    store, rank, _ = a_hbm.shape
    requests, devices = tokens_hbm.shape
    z, y, core = lax.axis_index("z"), lax.axis_index("y"), lax.axis_index("core")
    first_position = ((z * 2 + y) * 2 + core) * store
    tables = []
    for i, (src, dst) in enumerate(((home_hbm, home_ref), (adapter_hbm, adapter_ref), (tokens_hbm, tokens_ref))):
        tables.append(pltpu.make_async_copy(src, dst, table_sems.at[i]))
    own = pltpu.make_async_copy(x_hbm, x_ref, sems.at[2 * NAMED])
    for copy in (*tables, own):
        copy.start()
    for copy in tables:
        copy.wait()

    def slot_of(owner, i):
        return home_ref[adapter_ref[owner * requests + i]] - first_position

    def extremes(owner, carry):
        first, last = carry
        for i in range(requests):
            slot = slot_of(owner, i)
            here = (slot >= 0) & (slot < store)
            first = jnp.where(here, jnp.minimum(first, slot), first)
            last = jnp.where(here, jnp.maximum(last, slot), last)
        return first, last

    first, last = lax.fori_loop(0, devices, extremes, (jnp.int32(store - 1), jnp.int32(0)))
    copies = []
    for i, slot in enumerate((first, last)):
        rows = pl.ds(i * rank, rank)
        copies.append(pltpu.make_async_copy(a_hbm.at[slot], a_ref.at[rows], sems.at[2 * i]))
        copies.append(pltpu.make_async_copy(b_hbm.at[slot], b_ref.at[rows], sems.at[2 * i + 1]))
    for copy in copies:
        copy.start()

    def rows_of(owner, carry):
        block = (((owner // 4) ^ z) * 2 + ((owner % 2) ^ core)) * 2 + (((owner // 2) % 2) ^ y)
        places = lax.broadcasted_iota(jnp.int32, (tok_rows, 1), 0)
        wanted = jnp.full((tok_rows, 1), -1, jnp.int32)
        begin = jnp.int32(0)
        for i in range(requests):
            slot = slot_of(owner, i)
            one = jnp.where(slot == first, 0, jnp.where(slot == last, 1, -1))
            wanted = jnp.where(places >= begin, one, wanted)
            begin = begin + tokens_ref[i, owner]
        which_ref[pl.ds(pl.multiple_of(block * tok_rows, tok_rows), tok_rows), :] = wanted
        return carry

    lax.fori_loop(0, devices, rows_of, 0)
    for copy in (*copies, own):
        copy.wait()


def prepare(home, adapter, tokens, a, b, x, tok_rows):
    _, rank, width = a.shape
    rows = tokens.shape[0] * tok_rows
    sources = (home, adapter, tokens.T, a, b, x)
    return pl.pallas_call(
        functools.partial(prepare_kernel, tok_rows=tok_rows),
        out_shape=(
            VMEM((rows, 1), jnp.int32),
            VMEM((NAMED * rank, width), BF16),
            VMEM((NAMED * rank, width), BF16),
            VMEM(x.shape, BF16),
        ),
        in_specs=[FAR] * len(sources),
        out_specs=(WHOLE,) * 4,
        scratch_shapes=[pltpu.SMEM(v.shape, jnp.int32) for v in sources[:3]]
        + [pltpu.SemaphoreType.DMA((n,)) for n in (3, 2 * NAMED + 1)],
        compiler_params=PARAMS,
        cost_estimate=pl.CostEstimate(flops=0, bytes_accessed=4 << 20, transcendentals=0),
        name="prepare",
    )(*[pltpu.with_memory_space_constraint(v, pltpu.HBM) for v in sources])


def partial_kernel(which_ref, w_ref, a_ref, b_ref, *refs, parts, rank):
    xs, outs, x_ref = refs[: 4 * len(parts)], refs[4 * len(parts) : -1], refs[-1]
    tok_rows, width = xs[0].shape
    depth = w_ref.shape[0]
    step = 4096
    me = (lax.axis_index("z") * 2 + lax.axis_index("y")) * 2 + lax.axis_index("core")

    inputs = None
    for k in range(0, width, step):
        at = pl.ds(k, step)
        rows = jnp.concatenate([x[:, at].astype(F32) for x in xs], 0).astype(BF16)
        x_ref[:, at] = rows
        part = lax.dot_general(rows, a_ref[:, at], (((1,), (1,)), ((), ())), preferred_element_type=F32)
        inputs = part if inputs is None else inputs + part
    block = 4 * tok_rows
    which = jnp.concatenate([which_ref[pl.ds(s * block, block), :] for s in parts], 0)
    columns = lax.broadcasted_iota(jnp.int32, inputs.shape, 1) // rank
    inputs = jnp.where(columns == which, inputs, 0.0).astype(BF16)
    features = x_ref[:, pl.ds(pl.multiple_of(me * depth, depth), depth)]

    def body(i, carry):
        at = pl.ds(pl.multiple_of(i * step, step), step)
        total = jnp.dot(features, w_ref[:, at], preferred_element_type=F32)
        total += jnp.dot(inputs, b_ref[:, at], preferred_element_type=F32)
        half = block // 2
        for j in range(len(parts)):
            outs[2 * j][:, at] = total[j * block : j * block + half]
            outs[2 * j + 1][:, at] = total[j * block + half : (j + 1) * block].astype(BF16)
        return carry

    lax.fori_loop(0, width // step, body, 0)


def partial_rows(which, w, a, b, xs, parts, rank):
    rows, width = xs[0].shape
    which, a, b, *xs = [pltpu.with_memory_space_constraint(v, VMEM) for v in (which, a, b, *xs)]
    total = 4 * rows * len(parts)
    return pl.pallas_call(
        functools.partial(partial_kernel, parts=parts, rank=rank),
        out_shape=(VMEM((2 * rows, width), F32), VMEM((2 * rows, width), BF16)) * len(parts),
        in_specs=[WHOLE] * (4 + len(xs)),
        out_specs=(WHOLE,) * (2 * len(parts)),
        scratch_shapes=[VMEM((total, width), BF16)],
        compiler_params=PARAMS,
        cost_estimate=pl.CostEstimate(
            flops=2 * total * width * (w.shape[0] + 2 * a.shape[0]), bytes_accessed=16 << 20, transcendentals=0
        ),
        name="partial_rows",
    )(which, w, a, b, *xs)


def shards(attention_out, o_weight, a_down, b_up, adapter_home, req_adapter, req_tokens):
    tok_rows, width = attention_out.shape
    rank = a_down.shape[1]
    planes = lax.axis_size("z")
    which, a, b, own = prepare(adapter_home, req_adapter, req_tokens, a_down, b_up, attention_out, tok_rows)

    far = {0: attention_out, 1: across(attention_out, 1)}
    near = {0: other(attention_out, "y"), 1: diagonal(attention_out, 1)}
    for e in range(2, planes, 2):
        far[e] = across(attention_out, e)
        near[e] = other(after(far[e], which), "y")
        far[e + 1], near[e + 1] = across(far[e], 1), across(near[e], 1)

    parts = tuple(range(planes))[::-1]
    xs = []
    for e in parts:
        waits = near[e] if e != 1 else after(near[e], far[planes - 1])
        xs += [far[e] if e else own, near[e], other(far[e], "core"), other(waits, "core")]
    sums = partial_rows(which, o_weight, a, b, xs, parts, rank)
    out = None
    arriving = []
    before = ()
    for j, e in enumerate(parts):
        keep, got = sums[2 * j], other(sums[2 * j + 1], "core")
        here = keep[:tok_rows] + got[:tok_rows].astype(F32)
        there = (keep[tok_rows:] + got[tok_rows:].astype(F32)).astype(BF16)
        if e == 0:
            there = after(there, *before)
        received = other(there, "y")
        if e > 1:
            before = (received,)
        part = here + received.astype(F32)
        if e == 0:
            out = part
        else:
            arriving.append(across(part.astype(BF16), e))
    for part in arriving:
        out = out + part.astype(F32)
    return out.astype(BF16)


def solution(mesh):
    groups, wide = mesh.shape["groups"], mesh.shape["wide"]
    wide_axes = ("z", "y", "core")
    grid = Mesh(mesh.devices.reshape(groups, wide // 4, 2, 2), ("groups",) + wide_axes)
    every = ("groups",) + wide_axes
    in_specs = (
        P(every, None),
        P(wide_axes, None),
        P(every, None, None),
        P(every, None, None),
        P("groups"),
        P("groups"),
        P("groups", None),
    )
    return jax.shard_map(shards, mesh=grid, in_specs=in_specs, out_specs=P(every, None), check_vma=False)
```

```python
import functools

import jax
import jax.numpy as jnp
from jax import lax
from jax.experimental import pallas as pl
from jax.experimental.pallas import tpu as pltpu
from jax.sharding import Mesh, PartitionSpec as P

BF16 = jnp.bfloat16
F32 = jnp.float32
VMEM = pltpu.VMEM
SWAP = ((0, 1), (1, 0))
NAMED = 2
WHOLE = pl.BlockSpec(memory_space=VMEM)
SCALAR = pl.BlockSpec(memory_space=pltpu.SMEM)
FAR = pl.BlockSpec(memory_space=pltpu.HBM)
PARAMS = pltpu.CompilerParams(vmem_limit_bytes=24 << 20)


def other(x, axis):
    return lax.ppermute(x, axis, SWAP)


def across(x, away):
    return lax.ppermute(x, "z", [(i, i ^ away) for i in range(lax.axis_size("z"))])


def diagonal(x, away):
    places = [(i, j) for i in range(lax.axis_size("z")) for j in range(2)]
    return lax.ppermute(x, ("z", "y"), [(2 * i + j, 2 * (i ^ away) + 1 - j) for i, j in places])


def after(x, *others):
    return lax.optimization_barrier((x, *others))[0]


def prepare_kernel(
    home_hbm, adapter_hbm, tokens_hbm, a_hbm, b_hbm, x_hbm, which_ref, a_ref, b_ref, x_ref,
    home_ref, adapter_ref, tokens_ref, table_sems, sems, *, tok_rows,
):
    store, rank, _ = a_hbm.shape
    requests, devices = tokens_hbm.shape
    z, y, core = lax.axis_index("z"), lax.axis_index("y"), lax.axis_index("core")
    first_position = ((z * 2 + y) * 2 + core) * store
    tables = []
    for i, (src, dst) in enumerate(((home_hbm, home_ref), (adapter_hbm, adapter_ref), (tokens_hbm, tokens_ref))):
        tables.append(pltpu.make_async_copy(src, dst, table_sems.at[i]))
    own = pltpu.make_async_copy(x_hbm, x_ref, sems.at[2 * NAMED])
    for copy in tables:
        copy.start()
    for copy in tables:
        copy.wait()

    def slot_of(owner, i):
        return home_ref[adapter_ref[owner * requests + i]] - first_position

    def extremes(owner, carry):
        first, last = carry
        for i in range(requests):
            slot = slot_of(owner, i)
            here = (slot >= 0) & (slot < store)
            first = jnp.where(here, jnp.minimum(first, slot), first)
            last = jnp.where(here, jnp.maximum(last, slot), last)
        return first, last

    first, last = lax.fori_loop(0, devices, extremes, (jnp.int32(store - 1), jnp.int32(0)), unroll=4)
    copies = []
    for i, slot in enumerate((first, last)):
        rows = pl.ds(i * rank, rank)
        copies.append(pltpu.make_async_copy(a_hbm.at[slot], a_ref.at[rows], sems.at[2 * i]))
        copies.append(pltpu.make_async_copy(b_hbm.at[slot], b_ref.at[rows], sems.at[2 * i + 1]))
    for copy in (*copies, own):
        copy.start()

    def rows_of(owner, carry):
        block = (((owner // 4) ^ z) * 2 + ((owner % 2) ^ core)) * 2 + (((owner // 2) % 2) ^ y)
        places = lax.broadcasted_iota(jnp.int32, (tok_rows, 1), 0)
        wanted = jnp.full((tok_rows, 1), -1, jnp.int32)
        begin = jnp.int32(0)
        for i in range(requests):
            slot = slot_of(owner, i)
            one = jnp.where(slot == first, 0, jnp.where(slot == last, 1, -1))
            wanted = jnp.where(places >= begin, one, wanted)
            begin = begin + tokens_ref[i, owner]
        which_ref[pl.ds(pl.multiple_of(block * tok_rows, tok_rows), tok_rows), :] = wanted
        return carry

    lax.fori_loop(0, devices, rows_of, 0)
    for copy in (*copies, own):
        copy.wait()


def prepare(home, adapter, tokens, a, b, x, tok_rows):
    _, rank, width = a.shape
    rows = tokens.shape[0] * tok_rows
    sources = (home, adapter, tokens.T, a, b, x)
    return pl.pallas_call(
        functools.partial(prepare_kernel, tok_rows=tok_rows),
        out_shape=(
            VMEM((rows, 1), jnp.int32),
            VMEM((NAMED * rank, width), BF16),
            VMEM((NAMED * rank, width), BF16),
            VMEM(x.shape, BF16),
        ),
        in_specs=[FAR] * len(sources),
        out_specs=(WHOLE,) * 4,
        scratch_shapes=[pltpu.SMEM(v.shape, jnp.int32) for v in sources[:3]]
        + [pltpu.SemaphoreType.DMA((n,)) for n in (3, 2 * NAMED + 1)],
        compiler_params=PARAMS,
        cost_estimate=pl.CostEstimate(flops=0, bytes_accessed=4 << 20, transcendentals=0),
        name="prepare",
    )(*[pltpu.with_memory_space_constraint(v, pltpu.HBM) for v in sources])


def partial_kernel(which_ref, w_ref, a_ref, b_ref, *refs, parts, rank):
    xs, outs, x_ref = refs[: 4 * len(parts)], refs[4 * len(parts) : -1], refs[-1]
    tok_rows, width = xs[0].shape
    depth = w_ref.shape[0]
    step = 4096
    me = (lax.axis_index("z") * 2 + lax.axis_index("y")) * 2 + lax.axis_index("core")

    inputs = None
    for k in range(0, width, step):
        at = pl.ds(k, step)
        rows = jnp.concatenate([x[:, at].astype(F32) for x in xs], 0).astype(BF16)
        x_ref[:, at] = rows
        part = lax.dot_general(rows, a_ref[:, at], (((1,), (1,)), ((), ())), preferred_element_type=F32)
        inputs = part if inputs is None else inputs + part
    block = 4 * tok_rows
    which = jnp.concatenate([which_ref[pl.ds(s * block, block), :] for s in parts], 0)
    columns = lax.broadcasted_iota(jnp.int32, inputs.shape, 1) // rank
    inputs = jnp.where(columns == which, inputs, 0.0).astype(BF16)
    features = x_ref[:, pl.ds(pl.multiple_of(me * depth, depth), depth)]

    def body(i, carry):
        at = pl.ds(pl.multiple_of(i * step, step), step)
        total = jnp.dot(features, w_ref[:, at], preferred_element_type=F32)
        total += jnp.dot(inputs, b_ref[:, at], preferred_element_type=F32)
        half = block // 2
        for j in range(len(parts)):
            outs[2 * j][:, at] = total[j * block : j * block + half]
            outs[2 * j + 1][:, at] = total[j * block + half : (j + 1) * block].astype(BF16)
        return carry

    lax.fori_loop(0, width // step, body, 0)


def partial_rows(which, w, a, b, xs, parts, rank):
    rows, width = xs[0].shape
    which, a, b, *xs = [pltpu.with_memory_space_constraint(v, VMEM) for v in (which, a, b, *xs)]
    total = 4 * rows * len(parts)
    return pl.pallas_call(
        functools.partial(partial_kernel, parts=parts, rank=rank),
        out_shape=(VMEM((2 * rows, width), F32), VMEM((2 * rows, width), BF16)) * len(parts),
        in_specs=[WHOLE] * (4 + len(xs)),
        out_specs=(WHOLE,) * (2 * len(parts)),
        scratch_shapes=[VMEM((total, width), BF16)],
        compiler_params=PARAMS,
        cost_estimate=pl.CostEstimate(
            flops=2 * total * width * (w.shape[0] + 2 * a.shape[0]), bytes_accessed=16 << 20, transcendentals=0
        ),
        name="partial_rows",
    )(which, w, a, b, *xs)


def shards(attention_out, o_weight, a_down, b_up, adapter_home, req_adapter, req_tokens):
    tok_rows, width = attention_out.shape
    rank = a_down.shape[1]
    planes = lax.axis_size("z")
    which, a, b, own = prepare(adapter_home, req_adapter, req_tokens, a_down, b_up, attention_out, tok_rows)

    far = {0: attention_out, 1: across(attention_out, 1)}
    near = {0: other(attention_out, "y"), 1: diagonal(attention_out, 1)}
    for e in range(2, planes, 2):
        far[e] = across(attention_out, e)
        near[e] = other(after(far[e], which), "y")
        far[e + 1], near[e + 1] = across(far[e], 1), across(near[e], 1)

    parts = tuple(range(planes))[::-1]
    xs = []
    for e in parts:
        waits = near[e] if e != 1 else after(near[e], far[planes - 1])
        xs += [far[e] if e else own, near[e], other(far[e], "core"), other(waits, "core")]
    sums = partial_rows(which, o_weight, a, b, xs, parts, rank)
    out = None
    arriving = []
    before = ()
    for j, e in enumerate(parts):
        keep, got = sums[2 * j], other(sums[2 * j + 1], "core")
        here = keep[:tok_rows] + got[:tok_rows].astype(F32)
        there = (keep[tok_rows:] + got[tok_rows:].astype(F32)).astype(BF16)
        if e == 0:
            there = after(there, *before)
        received = other(there, "y")
        if e > 1:
            before = (received,)
        part = here + received.astype(F32)
        if e == 0:
            out = part
        else:
            arriving.append(across(part.astype(BF16), e))
    for part in arriving:
        out = out + part.astype(F32)
    return out.astype(BF16)


def solution(mesh):
    groups, wide = mesh.shape["groups"], mesh.shape["wide"]
    wide_axes = ("z", "y", "core")
    grid = Mesh(mesh.devices.reshape(groups, wide // 4, 2, 2), ("groups",) + wide_axes)
    every = ("groups",) + wide_axes
    in_specs = (
        P(every, None),
        P(wide_axes, None),
        P(every, None, None),
        P(every, None, None),
        P("groups"),
        P("groups"),
        P("groups", None),
    )
    return jax.shard_map(shards, mesh=grid, in_specs=in_specs, out_specs=P(every, None), check_vma=False)
```
